32 devices in a mesh: gy: 8 (over z, core), gz: 4 (over y, x).
Axes of the slice: x: 2, y: 2, z: 4, core: 2. Of those that a mesh axis runs over, the one named last changes fastest.
Arguments:
- volume: bfloat16 [4, 64, 32, 256], P(None, 'gy', 'gz'), may hold values from -6 to 6
- block_weight: bfloat16 [3, 3, 3, 256, 256], replicated, may hold values from -0.078125 to 0.078125
- aspp_weight: bfloat16 [3, 3, 3, 3, 256, 128], replicated, may hold values from -0.078125 to 0.078125
- proj_weight: bfloat16 [384, 128], replicated, may hold values from -0.3125 to 0.3125
- cotangent: bfloat16 [4, 64, 32, 128], P(None, 'gy', 'gz'), may hold values from -6 to 6
Outputs:
- pyramid_out: bfloat16 [4, 64, 32, 128], P(None, 'gy', 'gz')
- grad_volume: bfloat16 [4, 64, 32, 256], P(None, 'gy', 'gz')
- grad_block: float32 [1769472], P(('gy', 'gz'))
- grad_aspp: float32 [2654208], P(('gy', 'gz'))
- grad_proj: float32 [49152], P(('gy', 'gz'))
The draws below stay inside these ranges and needn't reach their ends.
All inputs are finite; a program needn't handle non-finite values.
Results may differ from the reference program's by a relative error of at most 0.01.
Values may be sent and summed in bfloat16 or wider, within the bound.
A program may use at most 192 MiB of HBM per device.

```python
import jax
import jax.numpy as jnp

C = 256
A = 128
X = 4
NY = 64
NZ = 32


def block_scale(key, dims, shards, least, high):
    gain, own = 1.0, jax.random.fold_in(key, 6)
    for axis_at, parts in shards:
        steps = jnp.exp(jax.random.uniform(jax.random.fold_in(own, axis_at), (parts,), jnp.float32, least / len(shards), high / len(shards)))
        gain = gain * jnp.repeat(steps, dims[axis_at] // parts).reshape([-1 if axis == axis_at else 1 for axis in range(len(dims))])
    return gain


def bell_draw(rng, extent, scale, bound, shards=(), kind=jnp.bfloat16):
    result = scale * jax.random.normal(rng, extent, jnp.float32)
    if shards:
        result = result * block_scale(rng, extent, shards, -0.22, 0.18)
    return jnp.clip(result, -bound, bound).astype(kind)


def setup_inputs(seed: int = 0) -> dict:
    key_of = jax.random.split(jax.random.key(seed), 6)
    return {
        "volume": bell_draw(key_of[0], (X, NY, NZ, C), 1.0, 6.0, ((1, 8), (2, 4))),
        "block_weight": bell_draw(key_of[1], (3, 3, 3, C, C), (27 * C) ** -0.5, 0.078125),
        "aspp_weight": bell_draw(key_of[2], (3, 3, 3, 3, C, A), (27 * C) ** -0.5, 0.078125),
        "proj_weight": bell_draw(key_of[3], (3 * A, A), (3 * A) ** -0.5, 0.3125),
        "cotangent": bell_draw(key_of[4], (X, NY, NZ, A), 1.0, 6.0, ((1, 8), (2, 4))),
    }


dilation_rates = (2, 4, 8)

def silu_slope(value):
    sigma = jax.nn.sigmoid(value)
    return sigma * (1.0 + value * (1.0 - sigma))

def tap_conv(padded, kernel, dilation):
    depth = padded.shape[0] - 2 * dilation
    rows = padded.shape[1] - 2 * dilation
    cols = padded.shape[2] - 2 * dilation
    in_width = padded.shape[3]
    out_width = kernel.shape[-1]
    total = jnp.zeros((depth * rows * cols, out_width), jnp.float32)
    for first in range(3):
        for second in range(3):
            for third in range(3):
                piece = padded[first * dilation:first * dilation + depth, second * dilation:second * dilation + rows, third * dilation:third * dilation + cols]
                total = total + jnp.dot(piece.reshape(-1, in_width), kernel[first, second, third], preferred_element_type=jnp.float32)
    return total.reshape(depth, rows, cols, out_width)

def weight_grad(padded, grad_out, dilation):
    depth, rows, cols, out_width = grad_out.shape
    in_width = padded.shape[3]
    grad_rows = grad_out.reshape(-1, out_width)
    taps = []
    for first in range(3):
        for second in range(3):
            for third in range(3):
                piece = padded[first * dilation:first * dilation + depth, second * dilation:second * dilation + rows, third * dilation:third * dilation + cols]
                taps.append(jnp.dot(piece.reshape(-1, in_width).T, grad_rows, preferred_element_type=jnp.float32))
    return jnp.stack(taps).reshape(3, 3, 3, in_width, out_width)

def flipped(kernel):
    return jnp.swapaxes(kernel[::-1, ::-1, ::-1], 3, 4)

def pad_all(source, dilation):
    return jnp.pad(source, ((dilation, dilation), (dilation, dilation), (dilation, dilation), (0, 0)))

def reference(volume, block_weight, aspp_weight, proj_weight, cotangent):
    volume_padded = pad_all(volume, 1)
    pre_block = tap_conv(volume_padded, block_weight, 1)
    hidden = jax.nn.silu(pre_block).astype(jnp.bfloat16)
    branch_list = []
    for branch, dilation in enumerate(dilation_rates):
        branch_list.append(tap_conv(pad_all(hidden, dilation), aspp_weight[branch], dilation))
    branch_pre = jnp.concatenate(branch_list, -1).reshape(-1, 3 * A)
    joined_rows = jax.nn.silu(branch_pre).astype(jnp.bfloat16)
    pyramid_out = jnp.dot(joined_rows, proj_weight, preferred_element_type=jnp.float32).reshape(X, NY, NZ, A).astype(jnp.bfloat16)
    grad_rows = cotangent.reshape(-1, A)
    grad_proj = jnp.dot(joined_rows.T, grad_rows, preferred_element_type=jnp.float32)
    proj_back = jnp.dot(grad_rows, proj_weight.T, preferred_element_type=jnp.float32)
    grad_joined = (proj_back * silu_slope(branch_pre)).astype(jnp.bfloat16).reshape(X, NY, NZ, 3 * A)
    grad_hidden = jnp.zeros((X, NY, NZ, C), jnp.float32)
    aspp_list = []
    for branch, dilation in enumerate(dilation_rates):
        grad_piece = grad_joined[..., branch * A:(branch + 1) * A]
        grad_hidden = grad_hidden + tap_conv(pad_all(grad_piece, dilation), flipped(aspp_weight[branch]), dilation)
        aspp_list.append(weight_grad(pad_all(hidden, dilation), grad_piece, dilation))
    grad_pre = (grad_hidden * silu_slope(pre_block)).astype(jnp.bfloat16)
    grad_volume = tap_conv(pad_all(grad_pre, 1), flipped(block_weight), 1).astype(jnp.bfloat16)
    grad_block = weight_grad(volume_padded, grad_pre, 1)
    return (pyramid_out, grad_volume, grad_block.reshape(-1), jnp.stack(aspp_list).reshape(-1), grad_proj.reshape(-1))
```

```python
import math

import jax
import jax.numpy as jnp
import numpy as np
from jax import lax
from jax.sharding import PartitionSpec as P

dilation_rates = (2, 4, 8)
both = ("gy", "gz")


def extended(cells, sides, width):
    for axis, dim in sides:
        count = lax.axis_size(axis)
        ends = count - 1
        head = lax.slice_in_dim(cells, 0, width, axis=dim)
        tail = lax.slice_in_dim(cells, cells.shape[dim] - width, cells.shape[dim], axis=dim)
        cells = jnp.concatenate(
            [
                lax.ppermute(tail, axis, [(i, (i + 1) % count) for i in range(ends)]),
                cells,
                lax.ppermute(head, axis, [((i + 1) % count, i) for i in range(ends)]),
            ],
            axis=dim,
        )
    return cells


def silu_slope(value):
    sigma = jax.nn.sigmoid(value)
    return sigma * (1.0 + value * (1.0 - sigma))


def depth_taps(dilation, depth):
    return [tap for tap in range(3) if abs(tap - 1) * dilation < depth]


def patches(wide, margin, dilation, shape, flip=False):
    depth, rows, cols = shape
    channels = wide.shape[-1]
    deep = jnp.pad(wide, ((dilation, dilation), (0, 0), (0, 0), (0, 0)))
    start = margin - dilation
    pieces = []
    for first in depth_taps(dilation, depth):
        for second in range(3):
            for third in range(3):
                a, b, c = (2 - first, 2 - second, 2 - third) if flip else (first, second, third)
                pieces.append(
                    deep[
                        a * dilation : a * dilation + depth,
                        start + b * dilation : start + b * dilation + rows,
                        start + c * dilation : start + c * dilation + cols,
                    ].reshape(-1, channels)
                )
    return jnp.concatenate(pieces, axis=1)


def dot32(lhs, rhs):
    return jnp.dot(lhs, rhs, preferred_element_type=jnp.float32)


def outer(lhs, rhs):
    return lax.dot_general(lhs, rhs, (((0,), (0,)), ((), ())), preferred_element_type=jnp.float32)


def bit_list(axis):
    return [(axis, bit) for bit in range(int(math.log2(lax.axis_size(axis))))]


def share_of(terms, order):
    sizes = {axis: lax.axis_size(axis) for axis in both}
    dims = [(axis, bit) for axis in both for bit in reversed(range(int(math.log2(sizes[axis]))))]
    held = terms.reshape((2,) * len(dims) + terms.shape[1:])
    left = list(dims)
    for step, (axis, bit) in enumerate(order):
        at = left.index((axis, bit))
        mine = (lax.axis_index(axis) >> bit) & 1
        low = lax.index_in_dim(held, 0, at, keepdims=False)
        high = lax.index_in_dim(held, 1, at, keepdims=False)
        keep = jnp.where(mine == 0, low, high)
        send = jnp.where(mine == 0, high, low)
        got = lax.ppermute(send, axis, [(i, i ^ (1 << bit)) for i in range(sizes[axis])])
        held = keep.astype(jnp.float32) + got.astype(jnp.float32)
        left.pop(at)
        if step < len(order) - 1:
            held = held.astype(jnp.bfloat16)
    return held


def spread(packed, runs, final_rows):
    ngy, ngz = lax.axis_size("gy"), lax.axis_size("gz")
    count = ngy * ngz
    rows = packed.shape[0]
    edges = []
    for start, target, length in runs:
        for source in range(count):
            lo, hi = max(start, source * rows), min(start + length, source * rows + rows)
            shift = target - start
            if lo >= hi:
                continue
            for owner in range((lo + shift) // final_rows, (hi - 1 + shift) // final_rows + 1):
                cut_lo = max(lo + shift, owner * final_rows) - shift
                cut_hi = min(hi + shift, (owner + 1) * final_rows) - shift
                edges.append((source, owner, cut_lo, cut_hi, shift))
    rounds = []
    for edge in edges:
        for group in rounds:
            if all(edge[0] != other[0] and edge[1] != other[1] for other in group):
                group.append(edge)
                break
        else:
            rounds.append([edge])
    me = lax.axis_index("gy") * ngz + lax.axis_index("gz")
    at = jnp.arange(rows, dtype=jnp.int32)[:, None]
    total = None
    for group in rounds:
        table = np.zeros((count, 3), np.int32)
        table[:, 2] = rows
        pairs = []
        for source, owner, lo, hi, shift in group:
            table[source, 0] = lo - source * rows
            table[source, 1] = hi - source * rows
            table[owner, 2] = rows + source * rows + shift - owner * final_rows
            pairs.append((source, owner))
        line = jnp.asarray(table)[me]
        send = jnp.where((at >= line[0]) & (at < line[1]), packed, 0.0)
        got = lax.ppermute(send, both, pairs)
        room = jnp.zeros((final_rows + 2 * rows, packed.shape[1]), packed.dtype)
        room = lax.dynamic_update_slice(room, got, (line[2], 0))[rows : rows + final_rows]
        total = room if total is None else total + room
    return total


def local(volume, block_weight, aspp_weight, proj_weight, cotangent):
    shape = volume.shape[:3]
    depth, row_count, col_count = shape
    channels = volume.shape[-1]
    branch_width = aspp_weight.shape[-1]
    widest_rate = max(dilation_rates)
    count = lax.axis_size("gy") * lax.axis_size("gz")
    sides = (("gy", 1), ("gz", 2))
    gy_bits, gz_bits = bit_list("gy"), bit_list("gz")

    taps = [depth_taps(dilation, depth) for dilation in dilation_rates]
    branch_weights = [
        aspp_weight[branch, taps[branch][0] : taps[branch][-1] + 1].reshape(-1, channels, branch_width)
        for branch in range(len(dilation_rates))
    ]
    back_weight = jnp.concatenate(
        [jnp.swapaxes(weight, 1, 2).reshape(-1, channels) for weight in branch_weights]
    )
    block_back = jnp.swapaxes(block_weight.reshape(-1, channels, channels), 1, 2).reshape(-1, channels)

    volume_taps = patches(extended(volume, sides, 1), 1, 1, shape)
    pre_block = dot32(volume_taps, block_weight.reshape(-1, channels))
    hidden = jax.nn.silu(pre_block).astype(jnp.bfloat16)
    hidden_wide = extended(hidden.reshape(*shape, channels), sides, widest_rate)
    hidden_taps = [patches(hidden_wide, widest_rate, dilation, shape) for dilation in dilation_rates]
    branch_pre = jnp.concatenate(
        [
            dot32(rows, weight.reshape(-1, branch_width))
            for rows, weight in zip(hidden_taps, branch_weights)
        ],
        -1,
    )
    joined = jax.nn.silu(branch_pre).astype(jnp.bfloat16)
    pyramid_out = dot32(joined, proj_weight).reshape(*shape, branch_width).astype(jnp.bfloat16)
    grad_rows = cotangent.reshape(-1, branch_width)
    proj_back = lax.dot_general(
        grad_rows, proj_weight, (((1,), (1,)), ((), ())), preferred_element_type=jnp.float32
    )
    grad_joined = (proj_back * silu_slope(branch_pre)).astype(jnp.bfloat16)
    grad_wide = extended(grad_joined.reshape(*shape, -1), sides, widest_rate)

    grad_proj = outer(joined, grad_rows).astype(jnp.bfloat16).reshape(count, -1, branch_width)
    grad_aspp = jnp.concatenate(
        [
            outer(rows, grad_joined[:, branch * branch_width : (branch + 1) * branch_width]).astype(jnp.bfloat16)
            for branch, rows in enumerate(hidden_taps)
        ]
    ).reshape(count, -1, branch_width)
    packed_rows = grad_aspp.shape[1]
    packed = share_of(jnp.concatenate([grad_aspp, grad_proj], 1), gy_bits[:1] + gz_bits + gy_bits[:0:-1])
    proj_share = packed[packed_rows:].reshape(-1)
    runs, start = [], 0
    for branch in range(len(dilation_rates)):
        length = len(taps[branch]) * 9 * channels
        runs.append((start, (branch * 27 + taps[branch][0] * 9) * channels, length))
        start += length
    aspp_share = spread(
        packed[:packed_rows], runs, len(dilation_rates) * 27 * channels // count
    ).reshape(-1)

    grad_taps = jnp.concatenate(
        [
            patches(
                grad_wide[..., branch * branch_width : (branch + 1) * branch_width],
                widest_rate,
                dilation,
                shape,
                flip=True,
            )
            for branch, dilation in enumerate(dilation_rates)
        ],
        1,
    )
    grad_hidden = dot32(grad_taps, back_weight)
    grad_pre = (grad_hidden * silu_slope(pre_block)).astype(jnp.bfloat16)
    grad_pre_rim = extended(grad_pre.reshape(*shape, channels), sides, 1)

    grad_block = outer(volume_taps, grad_pre).astype(jnp.bfloat16).reshape(count, -1, channels)
    half = grad_block.shape[1] // 2
    block_share = jnp.concatenate(
        [
            share_of(grad_block[:, :half], gy_bits[:1] + gz_bits + gy_bits[:0:-1]),
            share_of(grad_block[:, half:], gy_bits[:1] + gz_bits[::-1] + gy_bits[:0:-1]),
        ]
    ).reshape(-1)
    grad_volume = dot32(patches(grad_pre_rim, 1, 1, shape, flip=True), block_back)
    grad_volume = grad_volume.reshape(*shape, channels).astype(jnp.bfloat16)
    return (pyramid_out, grad_volume, block_share, aspp_share, proj_share)


def solution(mesh):
    in_specs = (P(None, "gy", "gz", None), P(), P(), P(), P(None, "gy", "gz", None))
    out_specs = (
        P(None, "gy", "gz", None),
        P(None, "gy", "gz", None),
        P(("gy", "gz")),
        P(("gy", "gz")),
        P(("gy", "gz")),
    )
    return jax.shard_map(local, mesh=mesh, in_specs=in_specs, out_specs=out_specs, check_vma=False)
```

```python
import functools
import math

import jax
import jax.numpy as jnp
import numpy as np
from jax import lax
from jax.experimental import pallas as pl
from jax.experimental.pallas import tpu as pltpu
from jax.sharding import PartitionSpec as P

dilation_rates = (2, 4, 8)
both = ("gy", "gz")
directions = ((-1, -1), (-1, 0), (-1, 1), (0, -1), (0, 1), (1, -1), (1, 0), (1, 1))
send_order = (0, 2, 5, 7, 1, 3, 4, 6)


def exchange_kernel(shared, extent, send_ref, out_ref, send_sem, recv_sem):
    here = (lax.axis_index("gy"), lax.axis_index("gz"))
    barrier = pltpu.get_barrier_semaphore()
    places = []
    for step in directions:
        place = tuple(at + by for at, by in zip(here, step))
        inside = None
        for at, by, size in zip(place, step, extent):
            if by:
                test = at >= 0 if by < 0 else at < size
                inside = test if inside is None else inside & test
        places.append((place, inside))

    for place, inside in places:

        @pl.when(inside)
        def _(place=place):
            pl.semaphore_signal(barrier, inc=1, device_id=place, device_id_type=pl.DeviceIdType.MESH)

    peers = 1
    for at, size in zip(here, extent):
        peers = peers * (1 + jnp.where(at > 0, 1, 0) + jnp.where(at < size - 1, 1, 0))
    pl.semaphore_wait(barrier, peers - 1)

    def copy(way, slot):
        return pltpu.make_async_remote_copy(
            src_ref=send_ref.at[0 if shared else way],
            dst_ref=out_ref.at[slot],
            send_sem=send_sem.at[way],
            recv_sem=recv_sem.at[slot],
            device_id=places[way][0],
            device_id_type=pl.DeviceIdType.MESH,
        )

    for way in send_order:

        @pl.when(places[way][1])
        def _(way=way):
            copy(way, 7 - way).start()

    for way in range(8):

        @pl.when(jnp.logical_not(places[way][1]))
        def _(way=way):
            out_ref[way] = jnp.zeros(out_ref.shape[1:], out_ref.dtype)

    for way in range(8):

        @pl.when(places[way][1])
        def _(way=way):
            copy(way, way).wait_recv()

    for way in range(8):

        @pl.when(places[way][1])
        def _(way=way):
            copy(way, 7 - way).wait_send()


def exchange(send, call):
    extent = (lax.axis_size("gy"), lax.axis_size("gz"))
    return pl.pallas_call(
        functools.partial(exchange_kernel, send.shape[0] == 1, extent),
        out_shape=jax.ShapeDtypeStruct((8, *send.shape[1:]), send.dtype),
        in_specs=[pl.BlockSpec(memory_space=pltpu.VMEM)],
        out_specs=pl.BlockSpec(memory_space=pltpu.VMEM),
        scratch_shapes=[pltpu.SemaphoreType.DMA((8,)), pltpu.SemaphoreType.DMA((8,))],
        compiler_params=pltpu.CompilerParams(
            collective_id=call, has_side_effects=True, vmem_limit_bytes=16 * 1024 * 1024
        ),
    )(send)


def ring_of(cells, width, call):
    depth, rows, cols, channels = cells.shape
    if width == 1:
        send = []
        for by_y, by_z in directions:
            piece = cells
            if by_y:
                piece = piece[:, :1] if by_y < 0 else piece[:, rows - 1 :]
            if by_z:
                piece = piece[:, :, :1] if by_z < 0 else piece[:, :, cols - 1 :]
            piece = piece.reshape(-1, channels)
            send.append(jnp.pad(piece, ((0, depth * max(rows, cols) - piece.shape[0]), (0, 0))))
        got = exchange(jnp.stack(send), call)
        high, wide = [rows if not by_y else 1 for by_y, _ in directions], [cols if not by_z else 1 for _, by_z in directions]
        got = [
            got[way, : depth * high[way] * wide[way]].reshape(depth, high[way], wide[way], channels)
            for way in range(8)
        ]
    else:
        got = exchange(cells.reshape(1, -1, channels), call)
        cut_y, cut_z = {-1: slice(rows - width, None), 0: slice(None), 1: slice(0, width)}, {
            -1: slice(cols - width, None), 0: slice(None), 1: slice(0, width)}
        got = [
            got[way].reshape(depth, rows, cols, channels)[:, cut_y[by_y], cut_z[by_z]]
            for way, (by_y, by_z) in enumerate(directions)
        ]
    got.insert(4, cells)
    return jnp.concatenate([jnp.concatenate(got[at : at + 3], 2) for at in (0, 3, 6)], 1)


def silu_slope(value):
    sigma = jax.nn.sigmoid(value)
    return sigma * (1.0 + value * (1.0 - sigma))


def depth_taps(dilation, depth):
    return [tap for tap in range(3) if abs(tap - 1) * dilation < depth]


def patches(wide, margin, dilation, shape, flip=False):
    depth, rows, cols = shape
    channels = wide.shape[-1]
    deep = jnp.pad(wide, ((dilation, dilation), (0, 0), (0, 0), (0, 0)))
    start = margin - dilation
    pieces = []
    for first in depth_taps(dilation, depth):
        for second in range(3):
            for third in range(3):
                a, b, c = (2 - first, 2 - second, 2 - third) if flip else (first, second, third)
                pieces.append(
                    deep[
                        a * dilation : a * dilation + depth,
                        start + b * dilation : start + b * dilation + rows,
                        start + c * dilation : start + c * dilation + cols,
                    ].reshape(-1, channels)
                )
    return jnp.concatenate(pieces, axis=1)


def dot32(lhs, rhs):
    return jnp.dot(lhs, rhs, preferred_element_type=jnp.float32)


def outer(lhs, rhs):
    return lax.dot_general(lhs, rhs, (((0,), (0,)), ((), ())), preferred_element_type=jnp.float32)


def bit_list(axis):
    return [(axis, bit) for bit in range(int(math.log2(lax.axis_size(axis))))]


def share_of(terms, order):
    sizes = {axis: lax.axis_size(axis) for axis in both}
    dims = [(axis, bit) for axis in both for bit in reversed(range(int(math.log2(sizes[axis]))))]
    held = terms.reshape((2,) * len(dims) + terms.shape[1:])
    left = list(dims)
    for step, (axis, bit) in enumerate(order):
        at = left.index((axis, bit))
        mine = (lax.axis_index(axis) >> bit) & 1
        low = lax.index_in_dim(held, 0, at, keepdims=False)
        high = lax.index_in_dim(held, 1, at, keepdims=False)
        keep = jnp.where(mine == 0, low, high)
        send = jnp.where(mine == 0, high, low)
        got = lax.ppermute(send, axis, [(i, i ^ (1 << bit)) for i in range(sizes[axis])])
        held = keep.astype(jnp.float32) + got.astype(jnp.float32)
        left.pop(at)
        if step < len(order) - 1:
            held = held.astype(jnp.bfloat16)
    return held


def spread(packed, runs, final_rows):
    ngy, ngz = lax.axis_size("gy"), lax.axis_size("gz")
    count = ngy * ngz
    rows = packed.shape[0]
    edges = []
    for start, target, length in runs:
        for source in range(count):
            lo, hi = max(start, source * rows), min(start + length, source * rows + rows)
            shift = target - start
            if lo >= hi:
                continue
            for owner in range((lo + shift) // final_rows, (hi - 1 + shift) // final_rows + 1):
                cut_lo = max(lo + shift, owner * final_rows) - shift
                cut_hi = min(hi + shift, (owner + 1) * final_rows) - shift
                edges.append((source, owner, cut_lo, cut_hi, shift))
    rounds = []
    for edge in edges:
        for group in rounds:
            if all(edge[0] != other[0] and edge[1] != other[1] for other in group):
                group.append(edge)
                break
        else:
            rounds.append([edge])
    me = lax.axis_index("gy") * ngz + lax.axis_index("gz")
    at = jnp.arange(rows, dtype=jnp.int32)[:, None]
    total = None
    for group in rounds:
        table = np.zeros((count, 3), np.int32)
        table[:, 2] = rows
        pairs = []
        for source, owner, lo, hi, shift in group:
            table[source, 0] = lo - source * rows
            table[source, 1] = hi - source * rows
            table[owner, 2] = rows + source * rows + shift - owner * final_rows
            pairs.append((source, owner))
        line = jnp.asarray(table)[me]
        send = jnp.where((at >= line[0]) & (at < line[1]), packed, 0.0)
        got = lax.ppermute(send, both, pairs)
        room = jnp.zeros((final_rows + 2 * rows, packed.shape[1]), packed.dtype)
        room = lax.dynamic_update_slice(room, got, (line[2], 0))[rows : rows + final_rows]
        total = room if total is None else total + room
    return total


def local(volume, block_weight, aspp_weight, proj_weight, cotangent):
    shape = volume.shape[:3]
    depth, row_count, col_count = shape
    channels = volume.shape[-1]
    branch_width = aspp_weight.shape[-1]
    widest_rate = max(dilation_rates)
    count = lax.axis_size("gy") * lax.axis_size("gz")
    gy_bits, gz_bits = bit_list("gy"), bit_list("gz")

    taps = [depth_taps(dilation, depth) for dilation in dilation_rates]
    branch_weights = [
        aspp_weight[branch, taps[branch][0] : taps[branch][-1] + 1].reshape(-1, channels, branch_width)
        for branch in range(len(dilation_rates))
    ]
    back_weight = jnp.concatenate(
        [jnp.swapaxes(weight, 1, 2).reshape(-1, channels) for weight in branch_weights]
    )
    block_back = jnp.swapaxes(block_weight.reshape(-1, channels, channels), 1, 2).reshape(-1, channels)

    volume_taps = patches(ring_of(volume, 1, 0), 1, 1, shape)
    pre_block = dot32(volume_taps, block_weight.reshape(-1, channels))
    hidden = jax.nn.silu(pre_block).astype(jnp.bfloat16)
    hidden_wide = ring_of(hidden.reshape(*shape, channels), widest_rate, 1)
    hidden_taps = [patches(hidden_wide, widest_rate, dilation, shape) for dilation in dilation_rates]
    branch_pre = jnp.concatenate(
        [
            dot32(rows, weight.reshape(-1, branch_width))
            for rows, weight in zip(hidden_taps, branch_weights)
        ],
        -1,
    )
    joined = jax.nn.silu(branch_pre).astype(jnp.bfloat16)
    pyramid_out = dot32(joined, proj_weight).reshape(*shape, branch_width).astype(jnp.bfloat16)
    grad_rows = cotangent.reshape(-1, branch_width)
    proj_back = lax.dot_general(
        grad_rows, proj_weight, (((1,), (1,)), ((), ())), preferred_element_type=jnp.float32
    )
    grad_joined = (proj_back * silu_slope(branch_pre)).astype(jnp.bfloat16)
    grad_wide = ring_of(grad_joined.reshape(*shape, 3 * branch_width), widest_rate, 2)

    grad_proj = outer(joined, grad_rows).astype(jnp.bfloat16).reshape(count, -1, branch_width)
    grad_aspp = jnp.concatenate(
        [
            outer(rows, grad_joined[:, branch * branch_width : (branch + 1) * branch_width]).astype(jnp.bfloat16)
            for branch, rows in enumerate(hidden_taps)
        ]
    ).reshape(count, -1, branch_width)
    packed_rows = grad_aspp.shape[1]
    packed = share_of(jnp.concatenate([grad_aspp, grad_proj], 1), gy_bits[:1] + gz_bits + gy_bits[:0:-1])
    proj_share = packed[packed_rows:].reshape(-1)
    runs, start = [], 0
    for branch in range(len(dilation_rates)):
        length = len(taps[branch]) * 9 * channels
        runs.append((start, (branch * 27 + taps[branch][0] * 9) * channels, length))
        start += length
    aspp_share = spread(
        packed[:packed_rows], runs, len(dilation_rates) * 27 * channels // count
    ).reshape(-1)

    grad_taps = jnp.concatenate(
        [
            patches(
                grad_wide[..., branch * branch_width : (branch + 1) * branch_width],
                widest_rate,
                dilation,
                shape,
                flip=True,
            )
            for branch, dilation in enumerate(dilation_rates)
        ],
        1,
    )
    grad_hidden = dot32(grad_taps, back_weight)
    grad_pre = (grad_hidden * silu_slope(pre_block)).astype(jnp.bfloat16)
    grad_pre_rim = ring_of(grad_pre.reshape(*shape, channels), 1, 3)

    grad_block = outer(volume_taps, grad_pre).astype(jnp.bfloat16).reshape(count, -1, channels)
    half = grad_block.shape[1] // 2
    block_share = jnp.concatenate(
        [
            share_of(grad_block[:, :half], gy_bits[:1] + gz_bits + gy_bits[:0:-1]),
            share_of(grad_block[:, half:], gy_bits[:1] + gz_bits[::-1] + gy_bits[:0:-1]),
        ]
    ).reshape(-1)
    grad_volume = dot32(patches(grad_pre_rim, 1, 1, shape, flip=True), block_back)
    grad_volume = grad_volume.reshape(*shape, channels).astype(jnp.bfloat16)
    return (pyramid_out, grad_volume, block_share, aspp_share, proj_share)


def solution(mesh):
    in_specs = (P(None, "gy", "gz", None), P(), P(), P(), P(None, "gy", "gz", None))
    out_specs = (
        P(None, "gy", "gz", None),
        P(None, "gy", "gz", None),
        P(("gy", "gz")),
        P(("gy", "gz")),
        P(("gy", "gz")),
    )
    return jax.shard_map(local, mesh=mesh, in_specs=in_specs, out_specs=out_specs, check_vma=False)
```

```python
import functools
import math

import jax
import jax.numpy as jnp
import numpy as np
from jax import lax
from jax.experimental import pallas as pl
from jax.experimental.pallas import tpu as pltpu
from jax.sharding import PartitionSpec as P

dilation_rates = (2, 4, 8)
both = ("gy", "gz")
directions = ((-1, -1), (-1, 0), (-1, 1), (0, -1), (0, 1), (1, -1), (1, 0), (1, 1))
send_order = (0, 2, 5, 7, 1, 3, 4, 6)


def exchange_kernel(shared, extent, send_ref, out_ref, send_sem, recv_sem):
    here = (lax.axis_index("gy"), lax.axis_index("gz"))
    barrier = pltpu.get_barrier_semaphore()
    places = []
    for step in directions:
        place = tuple(at + by for at, by in zip(here, step))
        inside = None
        for at, by, size in zip(place, step, extent):
            if by:
                test = at >= 0 if by < 0 else at < size
                inside = test if inside is None else inside & test
        places.append((place, inside))

    for place, inside in places:

        @pl.when(inside)
        def _(place=place):
            pl.semaphore_signal(barrier, inc=1, device_id=place, device_id_type=pl.DeviceIdType.MESH)

    peers = 1
    for at, size in zip(here, extent):
        peers = peers * (1 + jnp.where(at > 0, 1, 0) + jnp.where(at < size - 1, 1, 0))
    pl.semaphore_wait(barrier, peers - 1)

    def copy(way, slot):
        return pltpu.make_async_remote_copy(
            src_ref=send_ref.at[0 if shared else way],
            dst_ref=out_ref.at[slot],
            send_sem=send_sem.at[way],
            recv_sem=recv_sem.at[slot],
            device_id=places[way][0],
            device_id_type=pl.DeviceIdType.MESH,
        )

    for way in send_order:

        @pl.when(places[way][1])
        def _(way=way):
            copy(way, 7 - way).start()

    for way in range(8):

        @pl.when(jnp.logical_not(places[way][1]))
        def _(way=way):
            out_ref[way] = jnp.zeros(out_ref.shape[1:], out_ref.dtype)

    for way in range(8):

        @pl.when(places[way][1])
        def _(way=way):
            copy(way, way).wait_recv()

    for way in range(8):

        @pl.when(places[way][1])
        def _(way=way):
            copy(way, 7 - way).wait_send()


def exchange(send, call):
    extent = (lax.axis_size("gy"), lax.axis_size("gz"))
    return pl.pallas_call(
        functools.partial(exchange_kernel, send.shape[0] == 1, extent),
        out_shape=jax.ShapeDtypeStruct((8, *send.shape[1:]), send.dtype),
        in_specs=[pl.BlockSpec(memory_space=pltpu.VMEM)],
        out_specs=pl.BlockSpec(memory_space=pltpu.VMEM),
        scratch_shapes=[pltpu.SemaphoreType.DMA((8,)), pltpu.SemaphoreType.DMA((8,))],
        compiler_params=pltpu.CompilerParams(
            collective_id=call, has_side_effects=True, vmem_limit_bytes=16 * 1024 * 1024
        ),
    )(send)


def ring_of(cells, width, call):
    depth, rows, cols, channels = cells.shape
    if width == 1:
        send = []
        for by_y, by_z in directions:
            piece = cells
            if by_y:
                piece = piece[:, :1] if by_y < 0 else piece[:, rows - 1 :]
            if by_z:
                piece = piece[:, :, :1] if by_z < 0 else piece[:, :, cols - 1 :]
            piece = piece.reshape(-1, channels)
            send.append(jnp.pad(piece, ((0, depth * max(rows, cols) - piece.shape[0]), (0, 0))))
        got = exchange(jnp.stack(send), call)
        high, wide = [rows if not by_y else 1 for by_y, _ in directions], [cols if not by_z else 1 for _, by_z in directions]
        got = [
            got[way, : depth * high[way] * wide[way]].reshape(depth, high[way], wide[way], channels)
            for way in range(8)
        ]
    else:
        got = exchange(cells.reshape(1, -1, channels), call)
        cut_y, cut_z = {-1: slice(rows - width, None), 0: slice(None), 1: slice(0, width)}, {
            -1: slice(cols - width, None), 0: slice(None), 1: slice(0, width)}
        got = [
            got[way].reshape(depth, rows, cols, channels)[:, cut_y[by_y], cut_z[by_z]]
            for way, (by_y, by_z) in enumerate(directions)
        ]
    got.insert(4, cells)
    return jnp.concatenate([jnp.concatenate(got[at : at + 3], 2) for at in (0, 3, 6)], 1)


def silu_slope(value):
    sigma = jax.nn.sigmoid(value)
    return sigma * (1.0 + value * (1.0 - sigma))


def depth_taps(dilation, depth):
    return [tap for tap in range(3) if abs(tap - 1) * dilation < depth]


def patches(wide, margin, dilation, shape, flip=False):
    depth, rows, cols = shape
    channels = wide.shape[-1]
    deep = jnp.pad(wide, ((dilation, dilation), (0, 0), (0, 0), (0, 0)))
    start = margin - dilation
    pieces = []
    for first in depth_taps(dilation, depth):
        for second in range(3):
            for third in range(3):
                a, b, c = (2 - first, 2 - second, 2 - third) if flip else (first, second, third)
                pieces.append(
                    deep[
                        a * dilation : a * dilation + depth,
                        start + b * dilation : start + b * dilation + rows,
                        start + c * dilation : start + c * dilation + cols,
                    ].reshape(-1, channels)
                )
    return jnp.concatenate(pieces, axis=1)


def dot32(lhs, rhs):
    return jnp.dot(lhs, rhs, preferred_element_type=jnp.float32)


def outer(lhs, rhs):
    return lax.dot_general(lhs, rhs, (((0,), (0,)), ((), ())), preferred_element_type=jnp.float32)


def bit_list(axis):
    return [(axis, bit) for bit in range(int(math.log2(lax.axis_size(axis))))]


def halved(terms, order):
    sizes = {axis: lax.axis_size(axis) for axis in both}
    left = [(axis, bit) for axis in both for bit in reversed(range(int(math.log2(sizes[axis]))))]
    held = terms.reshape((2,) * len(left) + terms.shape[1:])
    for step, (axis, bit) in enumerate(order):
        at = left.index((axis, bit))
        mine = (lax.axis_index(axis) >> bit) & 1
        low = lax.index_in_dim(held, 0, at, keepdims=False)
        high = lax.index_in_dim(held, 1, at, keepdims=False)
        keep = jnp.where(mine == 0, low, high)
        send = jnp.where(mine == 0, high, low)
        got = lax.ppermute(send, axis, [(i, i ^ (1 << bit)) for i in range(sizes[axis])])
        held = keep.astype(jnp.float32) + got.astype(jnp.float32)
        left.pop(at)
        if step < len(order) - 1:
            held = held.astype(jnp.bfloat16)
        held = yield held


def finish(stages, held):
    while True:
        try:
            held = stages.send(held)
        except StopIteration:
            return held


fence = lax.optimization_barrier


def spread(packed, runs, final_rows):
    ngy, ngz = lax.axis_size("gy"), lax.axis_size("gz")
    count = ngy * ngz
    rows = packed.shape[0]
    edges = []
    for start, target, length in runs:
        for source in range(count):
            lo, hi = max(start, source * rows), min(start + length, source * rows + rows)
            shift = target - start
            if lo >= hi:
                continue
            for owner in range((lo + shift) // final_rows, (hi - 1 + shift) // final_rows + 1):
                cut_lo = max(lo + shift, owner * final_rows) - shift
                cut_hi = min(hi + shift, (owner + 1) * final_rows) - shift
                edges.append((source, owner, cut_lo, cut_hi, shift))
    rounds = []
    for edge in edges:
        for group in rounds:
            if all(edge[0] != other[0] and edge[1] != other[1] for other in group):
                group.append(edge)
                break
        else:
            rounds.append([edge])
    me = lax.axis_index("gy") * ngz + lax.axis_index("gz")
    at = jnp.arange(rows, dtype=jnp.int32)[:, None]
    total = None
    for group in rounds:
        table = np.zeros((count, 3), np.int32)
        table[:, 2] = rows
        pairs = []
        for source, owner, lo, hi, shift in group:
            table[source, 0] = lo - source * rows
            table[source, 1] = hi - source * rows
            table[owner, 2] = rows + source * rows + shift - owner * final_rows
            pairs.append((source, owner))
        line = jnp.asarray(table)[me]
        send = jnp.where((at >= line[0]) & (at < line[1]), packed, 0.0)
        got = lax.ppermute(send, both, pairs)
        room = jnp.zeros((final_rows + 2 * rows, packed.shape[1]), packed.dtype)
        room = lax.dynamic_update_slice(room, got, (line[2], 0))[rows : rows + final_rows]
        total = room if total is None else total + room
    return total


def local(volume, block_weight, aspp_weight, proj_weight, cotangent):
    shape = volume.shape[:3]
    depth, row_count, col_count = shape
    channels = volume.shape[-1]
    branch_width = aspp_weight.shape[-1]
    widest_rate = max(dilation_rates)
    count = lax.axis_size("gy") * lax.axis_size("gz")
    gy_bits, gz_bits = bit_list("gy"), bit_list("gz")

    taps = [depth_taps(dilation, depth) for dilation in dilation_rates]
    branch_weights = [
        aspp_weight[branch, taps[branch][0] : taps[branch][-1] + 1].reshape(-1, channels, branch_width)
        for branch in range(len(dilation_rates))
    ]
    back_weight = jnp.concatenate(
        [jnp.swapaxes(weight, 1, 2).reshape(-1, channels) for weight in branch_weights]
    )
    block_back = jnp.swapaxes(block_weight.reshape(-1, channels, channels), 1, 2).reshape(-1, channels)

    volume_taps = patches(ring_of(volume, 1, 0), 1, 1, shape)
    pre_block = dot32(volume_taps, block_weight.reshape(-1, channels))
    hidden = jax.nn.silu(pre_block).astype(jnp.bfloat16)
    hidden_wide = ring_of(hidden.reshape(*shape, channels), widest_rate, 1)
    hidden_taps = [patches(hidden_wide, widest_rate, dilation, shape) for dilation in dilation_rates]
    branch_pre = jnp.concatenate(
        [
            dot32(rows, weight.reshape(-1, branch_width))
            for rows, weight in zip(hidden_taps, branch_weights)
        ],
        -1,
    )
    joined = jax.nn.silu(branch_pre).astype(jnp.bfloat16)
    pyramid_out = dot32(joined, proj_weight).reshape(*shape, branch_width).astype(jnp.bfloat16)
    grad_rows = cotangent.reshape(-1, branch_width)
    proj_back = lax.dot_general(
        grad_rows, proj_weight, (((1,), (1,)), ((), ())), preferred_element_type=jnp.float32
    )
    grad_joined = (proj_back * silu_slope(branch_pre)).astype(jnp.bfloat16)
    grad_proj = outer(joined, grad_rows).astype(jnp.bfloat16).reshape(count, -1, branch_width)
    grad_aspp = jnp.concatenate(
        [
            outer(rows, grad_joined[:, branch * branch_width : (branch + 1) * branch_width]).astype(jnp.bfloat16)
            for branch, rows in enumerate(hidden_taps)
        ]
    ).reshape(count, -1, branch_width)
    packed_rows = grad_aspp.shape[1]
    packed_terms, grad_joined = fence((jnp.concatenate([grad_aspp, grad_proj], 1), grad_joined))
    packed_stages = halved(packed_terms, gy_bits[:1] + gz_bits + gy_bits[:0:-1])
    packed = next(packed_stages)
    grad_wide = ring_of(grad_joined.reshape(*shape, 3 * branch_width), widest_rate, 2)
    grad_wide, packed = fence((grad_wide, packed))
    packed = packed_stages.send(packed)

    grad_taps = jnp.concatenate(
        [
            patches(
                grad_wide[..., branch * branch_width : (branch + 1) * branch_width],
                widest_rate,
                dilation,
                shape,
                flip=True,
            )
            for branch, dilation in enumerate(dilation_rates)
        ],
        1,
    )
    grad_hidden, packed = fence((dot32(grad_taps, back_weight), packed))
    packed = packed_stages.send(packed)
    grad_pre = (grad_hidden * silu_slope(pre_block)).astype(jnp.bfloat16)
    grad_block = outer(volume_taps, grad_pre).astype(jnp.bfloat16).reshape(count, -1, channels)
    half = grad_block.shape[1] // 2
    grad_block, grad_pre = fence((grad_block, grad_pre))
    orders = (gy_bits[:1] + gz_bits + gy_bits[:0:-1], gy_bits[:1] + gz_bits[::-1] + gy_bits[:0:-1])
    first_stages = halved(grad_block[:, :half], orders[0])
    second_stages = halved(grad_block[:, half:], orders[1])
    first, second = next(first_stages), next(second_stages)
    grad_pre_rim = ring_of(grad_pre.reshape(*shape, channels), 1, 3)
    grad_pre_rim, first, second, packed = fence((grad_pre_rim, first, second, packed))
    first, second = first_stages.send(first), second_stages.send(second)
    packed = packed_stages.send(packed)
    rim_taps = patches(grad_pre_rim, 1, 1, shape, flip=True)
    rim_taps, first, second, packed = fence((rim_taps, first, second, packed))
    grad_volume = dot32(rim_taps, block_back)
    grad_volume = grad_volume.reshape(*shape, channels).astype(jnp.bfloat16)
    packed = finish(packed_stages, packed)
    block_share = jnp.concatenate([finish(first_stages, first), finish(second_stages, second)]).reshape(-1)
    proj_share = packed[packed_rows:].reshape(-1)
    runs, start = [], 0
    for branch in range(len(dilation_rates)):
        length = len(taps[branch]) * 9 * channels
        runs.append((start, (branch * 27 + taps[branch][0] * 9) * channels, length))
        start += length
    aspp_share = spread(
        packed[:packed_rows], runs, len(dilation_rates) * 27 * channels // count
    ).reshape(-1)
    return (pyramid_out, grad_volume, block_share, aspp_share, proj_share)


def solution(mesh):
    in_specs = (P(None, "gy", "gz", None), P(), P(), P(), P(None, "gy", "gz", None))
    out_specs = (
        P(None, "gy", "gz", None),
        P(None, "gy", "gz", None),
        P(("gy", "gz")),
        P(("gy", "gz")),
        P(("gy", "gz")),
    )
    return jax.shard_map(local, mesh=mesh, in_specs=in_specs, out_specs=out_specs, check_vma=False)
```
